512 devices in a mesh: seq: 8 (over z), batch: 16 (over y, core), mp: 4 (over x).
Axes of the slice: x: 4, y: 8, z: 8, core: 2. Of those that a mesh axis runs over, the one named last changes fastest.
Arguments:
- queries: bfloat16 [16, 4096, 2048], P('batch', 'seq', 'mp'), may hold values from -200 to 200
- neighbour_ids: int32 [16, 64, 2], P('batch', 'seq'), may hold values from 0 to 127, as said below
- encoded: bfloat16 [128, 128, 896], P('batch'), may hold values from -6 to 6
- key_weight: bfloat16 [896, 2048], P(None, 'mp'), may hold values from -0.1875 to 0.1875
- value_weight: bfloat16 [896, 2048], P(None, 'mp'), may hold values from -0.1875 to 0.1875
Outputs:
- attended: bfloat16 [16, 4096, 2048], P('batch', 'seq', 'mp')
The draws below stay inside these ranges and needn't reach their ends.
Inputs may be any that keep to these rules, and one draw needn't show every extreme that they name: `neighbour_ids`: the 16 neighbours named by the groups of one index of seq and batch name at most 2 neighbours held by one owner, and every such block reaches 2 for some owner.
All inputs are finite; a program needn't handle non-finite values.
Results may differ from the reference program's by a relative error of at most 0.011.
Values may be sent and summed in bfloat16 or wider, within the bound.
A program may use at most 64 MiB of HBM per device.

```python
import jax
import jax.numpy as jnp
from jax import lax

HEADS = 16
DH = 128
ENC = 896
GROUP = 64
NEIGH = 2
NLEN = 128
TOK_DEV = 512
SEQS = 16
SEQ_LEN = 4096
REQ = 16
CAP = 2
NB_DEV = 8
NEIGHBOURS = 128
N_BATCH = 16


def draw_queries(key, part):
    key = jax.random.fold_in(key, 5)
    key_base = jax.random.fold_in(key, 0)
    shape = (SEQS, SEQ_LEN, HEADS * DH)
    values = jnp.clip(jax.random.normal(key_base, shape, jnp.float32), -6.0, 6.0)
    return values.astype(jnp.bfloat16)


def draw_neighbour_ids(key, part):
    key = jax.random.fold_in(key, 11)
    key_noise, key_hot, key_rows, key_shuffle = jax.random.split(key, 4)
    seq_devices = SEQ_LEN // TOK_DEV
    blocks = SEQS * seq_devices
    chosen = REQ // CAP
    owner_index = jnp.arange(N_BATCH, dtype=jnp.int32)
    hot_owner = jax.random.randint(key_hot, (), 0, N_BATCH)
    noise = jax.random.randint(key_noise, (blocks, N_BATCH), 0, 4 * N_BATCH)
    bias = jnp.where(owner_index == hot_owner, 8 * N_BATCH, 0).astype(jnp.int32)
    score = (noise + bias[None, :]) * N_BATCH + owner_index[None, :]
    top_scores, chosen_owners = lax.top_k(score, chosen)
    owners_each = jnp.repeat(chosen_owners.astype(jnp.int32), CAP, axis=1)
    rows_each = jax.random.randint(key_rows, (blocks, REQ), 0, NB_DEV)
    shuffle_scores = jax.random.randint(key_shuffle, (blocks, REQ), 0, 1 << 20) * REQ + jnp.arange(REQ, dtype=jnp.int32)[None, :]
    positions = jnp.argsort(shuffle_scores, axis=1, stable=True)
    ids = jnp.take_along_axis(owners_each * NB_DEV + rows_each, positions, axis=1)
    return ids.reshape(SEQS, SEQ_LEN // GROUP, NEIGH).astype(jnp.int32)


def levels(own_key, dims, cuts, low, largest):
    def one(position, parts):
        draws = jax.random.uniform(jax.random.fold_in(jax.random.fold_in(own_key, 6), position), (parts,), jnp.float32, low / len(cuts), largest / len(cuts))
        return jnp.repeat(jnp.exp(draws), dims[position] // parts).reshape((-1,) + (1,) * (len(dims) - position - 1))

    gain = one(*cuts[0])
    for cut in cuts[1:]:
        gain = gain * one(*cut)
    return gain


def scatter_about(rng, dims, scale, reach, pieces=(), kind=jnp.bfloat16):
    drawn = jax.random.normal(rng, dims, jnp.float32) * scale
    if len(pieces) > 0:
        drawn = levels(rng, dims, pieces, -0.22, 0.18) * drawn
    return jnp.clip(drawn, min=-reach, max=reach).astype(kind)


def setup_inputs(seed: int = 0) -> dict:
    streams_of = jax.random.split(jax.random.key(seed), 6)
    queries = draw_queries(jax.random.fold_in(streams_of[5], 71), 0)
    neighbour_ids = draw_neighbour_ids(jax.random.fold_in(streams_of[5], 71), 0)
    encoded = scatter_about(streams_of[2], (NEIGHBOURS, NLEN, ENC), 1.0, 6.0, ((0, 16),))
    key_weight = scatter_about(streams_of[3], (ENC, HEADS * DH), ENC ** -0.5, 0.1875, ((1, 4),))
    value_weight = scatter_about(streams_of[4], (ENC, HEADS * DH), ENC ** -0.5, 0.1875, ((1, 4),))
    return {"queries": queries, "neighbour_ids": neighbour_ids, "encoded": encoded, "key_weight": key_weight, "value_weight": value_weight}


def attend_groups(group_queries, group_keys, group_values):
    scores = jnp.einsum("cqhd,ckhd->chqk", group_queries.astype(jnp.float32), group_keys.astype(jnp.float32)) * (DH ** -0.5)
    row_max = jnp.max(scores, axis=-1, keepdims=True)
    expon = jnp.exp(scores - row_max)
    weights = (expon / jnp.sum(expon, axis=-1, keepdims=True)).astype(jnp.bfloat16)
    mixed = jnp.einsum("chqk,ckhd->cqhd", weights.astype(jnp.float32), group_values.astype(jnp.float32))
    return mixed.astype(jnp.bfloat16)


def reference(queries, neighbour_ids, encoded, key_weight, value_weight):
    width = HEADS * DH
    flat_rows = encoded.reshape(NEIGHBOURS * NLEN, ENC)
    key_table = jnp.dot(flat_rows, key_weight, preferred_element_type=jnp.float32).astype(jnp.bfloat16).reshape(NEIGHBOURS, NLEN, width)
    value_table = jnp.dot(flat_rows, value_weight, preferred_element_type=jnp.float32).astype(jnp.bfloat16).reshape(NEIGHBOURS, NLEN, width)
    num_groups = SEQ_LEN // GROUP

    def one_sequence(pair):
        seq_queries, seq_ids = pair
        padding = jnp.zeros((GROUP - 1, width), seq_queries.dtype)
        shifted = jnp.concatenate([seq_queries[GROUP - 1:], padding], axis=0).reshape(num_groups, GROUP, HEADS, DH)
        flat_ids = seq_ids.reshape(-1)
        group_keys = key_table[flat_ids].reshape(num_groups, NEIGH * NLEN, HEADS, DH)
        group_values = value_table[flat_ids].reshape(num_groups, NEIGH * NLEN, HEADS, DH)
        mixed = attend_groups(shifted, group_keys, group_values).reshape(SEQ_LEN, width)
        return jnp.concatenate([jnp.zeros((GROUP - 1, width), mixed.dtype), mixed[:SEQ_LEN - GROUP + 1]], axis=0)

    return lax.map(one_sequence, (queries, neighbour_ids))
```

```python
import functools

import jax
import jax.numpy as jnp
from jax import lax
from jax.experimental import pallas as pl
from jax.experimental.pallas import tpu as pltpu
from jax.sharding import PartitionSpec as P

MESH = pl.DeviceIdType.MESH
DH = 128
COL = 128
Y_CHUNKS = (0, 1, 2, 3, 4, 5, 6)
ORDER = (0, 1, 2, 3, 4, 5, 6)
LOOK = 1


def exchange_kernel(
    ids, q_hbm, e_hbm, wk_hbm, wv_hbm, o_ref,
    q_raw, e_own, wk, wv, table, asked, asked_s, packed, wide, q_pad, q_in, o_out, o_in,
    keys, values, acc, half0, half1, r0, r1, r2, r3, r4, r5, r6,
    load_sem, tab_send, tab_recv, tab_local, y_send, y_recv,
    to_right, to_left, from_left, from_right, on_right, on_left, opp_left, opp_right, edge_send, edge_recv,
):
    recv = (r0, r1, r2, r3, r4, r5, r6)
    halves = (half0, half1)
    z = lax.axis_index("seq")
    b = lax.axis_index("batch")
    x = lax.axis_index("mp")
    rows = e_own.shape[1]
    part = 8 * rows
    right = (z, b, lax.rem(x + 1, 4))
    left = (z, b, lax.rem(x + 3, 4))
    ahead = (lax.rem(z + 1, 8), b, x)
    behind = (lax.rem(z + 7, 8), b, x)

    def line(k):
        return lax.rem(b + k, 16)

    barrier = pltpu.get_barrier_semaphore()
    for device in (right, left, ahead, behind):
        pl.semaphore_signal(barrier, inc=1, device_id=device, device_id_type=MESH)

    def greet(k, carry):
        pl.semaphore_signal(barrier, inc=1, device_id=(z, line(k), x), device_id_type=MESH)
        return carry

    lax.fori_loop(1, 16, greet, 0)

    loads = [
        pltpu.make_async_copy(e_hbm.at[:, pl.ds(pl.multiple_of(x * rows, rows), rows), :], e_own, load_sem.at[0]),
        pltpu.make_async_copy(q_hbm.at[0], q_raw, load_sem.at[1]),
        pltpu.make_async_copy(wk_hbm, wk, load_sem.at[2]),
        pltpu.make_async_copy(wv_hbm, wv, load_sem.at[3]),
    ]
    for copy in loads:
        copy.start()

    lane = lax.broadcasted_iota(jnp.int32, (1, 128), 1)
    lane_owner = lax.shift_right_logical(lane, 1)
    lane_slot = lane & 1
    count = jnp.zeros((1, 128), jnp.int32)
    wanted = jnp.zeros((1, 128), jnp.int32)
    owners = []
    slot_of = []
    for s in range(16):
        one = ids[0, s // 2, s % 2]
        owner = lax.shift_right_logical(one, 3)
        same = lane_owner == owner
        wanted = jnp.where(same & (count == lane_slot), one & 7, wanted)
        count = count + same.astype(jnp.int32)
        rank = jnp.int32(0)
        for other in owners:
            rank = rank + (other == owner).astype(jnp.int32)
        owners.append(owner)
        slot_of.append(owner * 2 + jnp.minimum(rank, 1))
    table[...] = wanted

    loads[1].wait()
    wide[0:8, :] = jnp.zeros((8, wide.shape[1]), jnp.float32)
    wide[520:584, :] = jnp.zeros((64, wide.shape[1]), jnp.float32)
    for i in range(8):
        wide[8 + 64 * i : 72 + 64 * i, :] = q_raw[64 * i : 64 * i + 64, :].astype(jnp.float32)
    for i in range(9):
        q_pad[64 * i : 64 * i + 64, :] = wide[7 + 64 * i : 71 + 64 * i, :].astype(jnp.bfloat16)
    loads[0].wait()

    pl.semaphore_wait(barrier, 19)

    def tell(k, carry):
        pltpu.make_async_remote_copy(
            src_ref=table, dst_ref=asked.at[b], send_sem=tab_send, recv_sem=tab_recv,
            device_id=(z, line(k), x), device_id_type=MESH,
        ).start()
        return carry

    lax.fori_loop(1, 16, tell, 0)
    pltpu.make_async_copy(table, asked.at[b], tab_recv).start()
    edge_q = pltpu.make_async_remote_copy(
        src_ref=q_pad.at[pl.ds(0, 64)], dst_ref=q_in, send_sem=edge_send.at[0], recv_sem=edge_recv.at[0],
        device_id=behind, device_id_type=MESH,
    )
    edge_q.start()
    pltpu.make_async_copy(asked, asked, tab_recv).wait()
    to_scalar = pltpu.make_async_copy(asked, asked_s, tab_local)
    to_scalar.start()
    to_scalar.wait()

    for j in Y_CHUNKS:
        def serve(k, carry, j=j):
            to = line(k)
            for t in range(2):
                row = asked_s[to, 0, 2 * b + t]
                packed[j, k, t] = e_own[row, :, COL * j : COL * j + COL]
            pltpu.make_async_remote_copy(
                src_ref=packed.at[j, k], dst_ref=recv[j].at[pl.ds(2 * b, 2)],
                send_sem=y_send.at[j], recv_sem=y_recv.at[j],
                device_id=(z, to, x), device_id_type=MESH,
            ).start()
            return carry

        for t in range(2):
            row = asked_s[b, 0, 2 * b + t]
            packed[j, 0, t] = e_own[row, :, COL * j : COL * j + COL]
        pltpu.make_async_copy(packed.at[j, 0], recv[j].at[pl.ds(2 * b, 2)], y_recv.at[j]).start()
        lax.fori_loop(1, 16, serve, 0)

    units = [(h, j) for j in ORDER for h in (0, 1)]
    column = {j: pl.ds(COL * j, COL) for j in range(7)}

    def x_copy(h, j, src_row, dst_row, count, send, rcv, device):
        n = 7 * h + j
        return pltpu.make_async_remote_copy(
            src_ref=halves[h].at[pl.ds(src_row, count), column[j]],
            dst_ref=halves[h].at[pl.ds(dst_row, count), column[j]],
            send_sem=send.at[n], recv_sem=rcv.at[n], device_id=device, device_id_type=MESH,
        )

    def hop_right(h, j):
        return x_copy(h, j, 0, part, part, to_right, from_left, right)

    def hop_left(h, j):
        return x_copy(h, j, 0, 2 * part, part, to_left, from_right, left)

    def pass_right(h, j):
        return x_copy(h, j, part, 3 * part, part // 2, on_right, opp_left, right)

    def pass_left(h, j):
        return x_copy(h, j, 2 * part + part // 2, 3 * part + part // 2, part // 2, on_left, opp_right, left)

    def select_and_send(h, j):
        for s in range(8):
            slot = slot_of[8 * (1 - h) + s]
            halves[h][rows * s : rows * s + rows, COL * j : COL * j + COL] = recv[j][slot]
        hop_right(h, j).start()
        hop_left(h, j).start()

    def pass_on(h, j):
        hop_right(h, j).wait_recv()
        pass_right(h, j).start()
        hop_left(h, j).wait_recv()
        pass_left(h, j).start()

    def landed(h, j):
        pass_right(h, j).wait_recv()
        pass_left(h, j).wait_recv()

    group0 = (4, 0)

    def project_first(h):
        if h == 0:
            loads[2].wait()
            loads[3].wait()

        def body(i, carry):
            r = pl.ds(pl.multiple_of(i * part, part), part)
            lhs = halves[h][r, 0 : COL * 6]
            acc[h, r, 0:512] = jnp.dot(lhs, wk[0 : COL * 6, :], preferred_element_type=jnp.float32)
            acc[h, r, 512:1024] = jnp.dot(lhs, wv[0 : COL * 6, :], preferred_element_type=jnp.float32)
            return carry

        lax.fori_loop(0, 4, body, 0)

    def project_last(h):
        def body(i, carry):
            r = pl.ds(pl.multiple_of(i * part, part), part)
            to = pl.ds(pl.multiple_of(i * 2 * rows, 2 * rows), 2 * rows)
            lhs = halves[h][r, COL * 6 : COL * 7]
            k = acc[h, r, 0:512] + jnp.dot(lhs, wk[COL * 6 : COL * 7, :], preferred_element_type=jnp.float32)
            v = acc[h, r, 512:1024] + jnp.dot(lhs, wv[COL * 6 : COL * 7, :], preferred_element_type=jnp.float32)
            k = k.astype(jnp.bfloat16)
            v = v.astype(jnp.bfloat16)
            for g in range(4):
                keys[group0[h] + g, to, :] = k[2 * rows * g : 2 * rows * (g + 1), :]
                values[group0[h] + g, to, :] = v[2 * rows * g : 2 * rows * (g + 1), :]
            return carry

        lax.fori_loop(0, 4, body, 0)

    def attend(h):
        def body(i, carry):
            g = i + group0[h]
            r = pl.ds(pl.multiple_of(64 * g + 64, 64), 64)
            for n in range(4):
                c = slice(DH * n, DH * n + DH)
                scores = lax.dot_general(
                    q_pad[r, c], keys[g, :, c], (((1,), (1,)), ((), ())), preferred_element_type=jnp.float32
                ) * DH ** (-0.5)
                expon = jnp.exp(scores - jnp.max(scores, axis=-1, keepdims=True))
                weights = expon * (1.0 / jnp.sum(expon, axis=-1, keepdims=True))
                wide[r, c] = jnp.dot(
                    weights.astype(jnp.bfloat16), values[g, :, c], preferred_element_type=jnp.float32
                )
            return carry

        lax.fori_loop(0, 4, body, 0)

    edge_o = pltpu.make_async_remote_copy(
        src_ref=o_out, dst_ref=o_in, send_sem=edge_send.at[1], recv_sem=edge_recv.at[1],
        device_id=ahead, device_id_type=MESH,
    )

    def finish_half0():
        edge_q.wait_recv()
        row = lax.broadcasted_iota(jnp.int32, (64, 512), 0)
        q_pad[512:576, :] = jnp.where(
            row == 0, q_pad[512:576, :].astype(jnp.float32), q_in[...].astype(jnp.float32)
        ).astype(jnp.bfloat16)
        attend(0)
        o_out[...] = wide[512:576, :].astype(jnp.bfloat16)
        edge_o.start()

    done = {0: 0, 1: 0}

    def after(h, j):
        landed(h, j)
        done[h] += 1
        if done[h] == 6:
            project_first(h)
        if done[h] == 7:
            project_last(h)
            if h == 0:
                finish_half0()
            else:
                attend(1)

    seen = set()
    for n in range(len(units) + 2 * LOOK):
        if n < len(units):
            h, j = units[n]
            if j not in seen:
                seen.add(j)
                pltpu.make_async_copy(recv[j], recv[j], y_recv.at[j]).wait()
            select_and_send(h, j)
        if 0 <= n - LOOK < len(units):
            pass_on(*units[n - LOOK])
        if 0 <= n - 2 * LOOK < len(units):
            after(*units[n - 2 * LOOK])

    edge_o.wait_recv()
    wide[0:64, :] = jnp.where(z == 0, 0.0, o_in[...].astype(jnp.float32))
    for i in range(8):
        o_ref[0, 64 * i : 64 * i + 64, :] = wide[64 * i + 1 : 64 * i + 65, :].astype(jnp.bfloat16)

    edge_q.wait_send()
    edge_o.wait_send()
    pltpu.make_async_copy(asked.at[pl.ds(0, 15)], asked.at[pl.ds(0, 15)], tab_send).wait()
    for j in Y_CHUNKS:
        pltpu.make_async_copy(packed.at[j, pl.ds(0, 15)], packed.at[j, pl.ds(0, 15)], y_send.at[j]).wait()
    for h, j in units:
        hop_right(h, j).wait_send()
        hop_left(h, j).wait_send()
        pass_right(h, j).wait_send()
        pass_left(h, j).wait_send()


def local(queries, neighbour_ids, encoded, key_weight, value_weight):
    bf16, f32, i32 = jnp.bfloat16, jnp.float32, jnp.int32
    hbm = pl.BlockSpec(memory_space=pl.ANY)
    dma = pltpu.SemaphoreType.DMA
    return pl.pallas_call(
        exchange_kernel,
        out_shape=jax.ShapeDtypeStruct(queries.shape, bf16),
        in_specs=[pl.BlockSpec(memory_space=pltpu.SMEM), hbm, hbm, hbm, hbm],
        out_specs=pl.BlockSpec(memory_space=pltpu.VMEM),
        scratch_shapes=[
            pltpu.VMEM((512, 512), bf16),
            pltpu.VMEM((8, 32, 896), bf16),
            pltpu.VMEM((896, 512), bf16),
            pltpu.VMEM((896, 512), bf16),
            pltpu.VMEM((1, 128), i32),
            pltpu.VMEM((16, 1, 128), i32),
            pltpu.SMEM((16, 1, 128), i32),
            pltpu.VMEM((7, 16, 2, 32, 128), bf16),
            pltpu.VMEM((584, 512), f32),
            pltpu.VMEM((576, 512), bf16),
            pltpu.VMEM((64, 512), bf16),
            pltpu.VMEM((64, 512), bf16),
            pltpu.VMEM((64, 512), bf16),
            pltpu.VMEM((8, 256, 512), bf16),
            pltpu.VMEM((8, 256, 512), bf16),
            pltpu.VMEM((2, 1024, 1024), f32),
            pltpu.VMEM((1024, 896), bf16),
            pltpu.VMEM((1024, 896), bf16),
        ]
        + [pltpu.VMEM((32, 32, 128), bf16) for _ in range(7)]
        + [dma((4,)), dma, dma, dma, dma((7,)), dma((7,))]
        + [dma((14,)) for _ in range(8)]
        + [dma((2,)), dma((2,))],
        compiler_params=pltpu.CompilerParams(
            collective_id=0, has_side_effects=True, vmem_limit_bytes=48 * 2**20
        ),
        cost_estimate=pl.CostEstimate(flops=4_100_000_000, bytes_accessed=6_000_000, transcendentals=600_000),
    )(neighbour_ids, queries, encoded, key_weight, value_weight)


def solution(mesh):
    return jax.shard_map(
        local,
        mesh=mesh,
        in_specs=(
            P("batch", "seq", "mp"),
            P("batch", "seq", None),
            P("batch", None, None),
            P(None, "mp"),
            P(None, "mp"),
        ),
        out_specs=P("batch", "seq", "mp"),
        check_vma=False,
    )
```

```python
import jax
import jax.numpy as jnp
from jax import lax
from jax.experimental import pallas as pl
from jax.experimental.pallas import tpu as pltpu
from jax.sharding import PartitionSpec as P

MESH = pl.DeviceIdType.MESH
DH = 128
EXP2_SCALE = DH ** (-0.5) * 1.4426950408889634
COL = 128
Z_CHUNKS = (3, 4, 5)
Z_FIRST = 3
SERVE = (0, 1, 3, 2, 4, 5, 6)
UPFRONT = 3
PARTS = ((4, 5, 6, 7), (0, 1, 2, 3))
UNITS = (
    (0, 0), (1, 0), (0, 1), (0, 3), (1, 1), (0, 2), (1, 3), (0, 4), (0, 5), (0, 6), (1, 2), (1, 4), (1, 5), (1, 6),
)
LOOK = 3


def exchange_kernel(
    ids, q_hbm, e_hbm, wk_hbm, wv_hbm, o_ref,
    q_raw, e_own, e_line, wk, wv, table, asked_y, asked_z, asked_y_s, asked_z_s, packed, wide, q_pad, q_in, o_out, o_in,
    keys, values, scores, weights, acc0, acc1, part0, part1, r0, r1, r2, r3, r4, r5, r6,
    load_sem, tab_send, tab_recv, tab_local, pre_send, pre_recv, serve_send, serve_recv,
    to_right, to_left, from_left, from_right, on_right, on_left, opp_left, opp_right, edge_send, edge_recv,
):
    recv = (r0, r1, r2, r3, r4, r5, r6)
    parts = (part0, part1)
    accs = (acc0, acc1)
    z = lax.axis_index("seq")
    b = lax.axis_index("batch")
    x = lax.axis_index("mp")
    y = lax.div(b, 2)
    core = lax.rem(b, 2)
    zc = 2 * z + core
    rows = e_own.shape[1]
    right = (z, b, lax.rem(x + 1, 4))
    left = (z, b, lax.rem(x + 3, 4))
    ahead = (lax.rem(z + 1, 8), b, x)
    behind = (lax.rem(z + 7, 8), b, x)

    def y_line(k):
        to = lax.rem(b + k, 16)
        return to, (z, to, x)

    def z_line(k):
        to = lax.rem(zc + k, 16)
        return to, (lax.div(to, 2), 2 * y + lax.rem(to, 2), x)

    barrier = pltpu.get_barrier_semaphore()

    def greet_one(device):
        pl.semaphore_signal(barrier, inc=1, device_id=device, device_id_type=MESH)

    greet_one(right)
    greet_one(left)

    def greet(k, carry):
        greet_one(y_line(k)[1])
        greet_one(z_line(k)[1])
        return carry

    lax.fori_loop(1, 16, greet, 0)

    def greet_source(k, carry):
        greet_one((lax.rem(z + k, 8), zc, x))
        return carry

    lax.fori_loop(1, 8, greet_source, 0)

    @pl.when(y != z)
    def _():
        greet_one((z, zc, x))

    loads = [
        pltpu.make_async_copy(e_hbm.at[:, pl.ds(pl.multiple_of(x * rows, rows), rows), :], e_own, load_sem.at[0]),
        pltpu.make_async_copy(q_hbm.at[0], q_raw, load_sem.at[1]),
        pltpu.make_async_copy(wk_hbm, wk, load_sem.at[2]),
        pltpu.make_async_copy(wv_hbm, wv, load_sem.at[3]),
    ]
    for copy in loads:
        copy.start()

    lane = lax.broadcasted_iota(jnp.int32, (1, 128), 1)
    lane_owner = lax.shift_right_logical(lane, 1)
    lane_slot = lane & 1
    count = jnp.zeros((1, 128), jnp.int32)
    wanted = jnp.zeros((1, 128), jnp.int32)
    owners = []
    slot_of = []
    for s in range(16):
        one = ids[0, s % 2, s // 2]
        owner = lax.shift_right_logical(one, 3)
        same = lane_owner == owner
        wanted = jnp.where(same & (count == lane_slot), one & 7, wanted)
        count = count + same.astype(jnp.int32)
        rank = jnp.int32(0)
        for other in owners:
            rank = rank + (other == owner).astype(jnp.int32)
        owners.append(owner)
        slot_of.append(owner * 2 + jnp.minimum(rank, 1))
    table[...] = wanted
    loads[0].wait()

    pl.semaphore_wait(barrier, 39 + (y != z).astype(jnp.int32))

    def tell(line, asked, n, me):
        def body(k, carry):
            pltpu.make_async_remote_copy(
                src_ref=table, dst_ref=asked.at[me], send_sem=tab_send.at[n], recv_sem=tab_recv.at[n],
                device_id=line(k)[1], device_id_type=MESH,
            ).start()
            return carry

        lax.fori_loop(1, 16, body, 0)
        pltpu.make_async_copy(table, asked.at[me], tab_recv.at[n]).start()

    tell(y_line, asked_y, 0, b)
    tell(z_line, asked_z, 1, zc)

    z_cols = pl.ds(COL * Z_FIRST, COL * len(Z_CHUNKS))

    def spread(k, send):
        return pltpu.make_async_remote_copy(
            src_ref=e_own.at[z, :, z_cols], dst_ref=e_line.at[z], send_sem=pre_send.at[send], recv_sem=pre_recv,
            device_id=(y, 2 * lax.rem(y + k, 8) + core, x), device_id_type=MESH,
        )

    def spread_one(k, carry):
        spread(k, 0).start()
        return carry

    lax.fori_loop(1, 8, spread_one, 0)

    @pl.when(y != z)
    def _():
        spread(0, 1).start()

    @pl.when(y == z)
    def _():
        pltpu.make_async_copy(e_own.at[z, :, z_cols], e_line.at[z], pre_recv).start()

    loads[1].wait()
    wide[0:8, :] = jnp.zeros((8, wide.shape[1]), jnp.float32)
    wide[520:584, :] = jnp.zeros((64, wide.shape[1]), jnp.float32)
    for i in range(8):
        wide[8 + 64 * i : 72 + 64 * i, :] = q_raw[64 * i : 64 * i + 64, :].astype(jnp.float32)
    for i in range(9):
        q_pad[64 * i : 64 * i + 64, :] = wide[7 + 64 * i : 71 + 64 * i, :].astype(jnp.bfloat16)
    edge_q = pltpu.make_async_remote_copy(
        src_ref=q_pad.at[pl.ds(0, 64)], dst_ref=q_in, send_sem=edge_send.at[0], recv_sem=edge_recv.at[0],
        device_id=behind, device_id_type=MESH,
    )
    edge_q.start()
    for g in range(8):
        for m in range(4):
            values[g, :, 2 * DH * m + DH : 2 * DH * m + 2 * DH] = jnp.ones((256, DH), jnp.bfloat16)
    scalars = []
    for n, (asked, asked_s) in enumerate(((asked_y, asked_y_s), (asked_z, asked_z_s))):
        pltpu.make_async_copy(asked, asked, tab_recv.at[n]).wait()
        scalars.append(pltpu.make_async_copy(asked, asked_s, tab_local.at[n]))
        scalars[n].start()
    scalars[0].wait()

    def serve(j):
        if j in Z_CHUNKS:
            block, col, asked_s, me, line = e_line, COL * (j - Z_FIRST), asked_z_s, zc, z_line
            if j == Z_CHUNKS[0]:
                scalars[1].wait()
                pltpu.make_async_copy(e_line, e_line, pre_recv).wait()
        else:
            block, col, asked_s, me, line = e_own, COL * j, asked_y_s, b, y_line

        def pack(k, to):
            for t in range(2):
                packed[j, k, t] = block[asked_s[to, 0, 2 * me + t], :, col : col + COL]

        def body(k, carry):
            to, device = line(k)
            pack(k, to)
            pltpu.make_async_remote_copy(
                src_ref=packed.at[j, k], dst_ref=recv[j].at[pl.ds(2 * me, 2)],
                send_sem=serve_send.at[j], recv_sem=serve_recv.at[j], device_id=device, device_id_type=MESH,
            ).start()
            return carry

        lax.fori_loop(1, 16, body, 0)
        pack(0, me)
        pltpu.make_async_copy(packed.at[j, 0], recv[j].at[pl.ds(2 * me, 2)], serve_recv.at[j]).start()

    def x_copy(p, j, src_row, dst_row, count, send, rcv, device):
        return pltpu.make_async_remote_copy(
            src_ref=parts[p].at[j, pl.ds(src_row, count)],
            dst_ref=parts[p].at[j, pl.ds(dst_row, count)],
            send_sem=send.at[p, j], recv_sem=rcv.at[p, j], device_id=device, device_id_type=MESH,
        )

    def quarter(p):
        return 2 * rows * len(PARTS[p])

    def hop_right(p, j):
        return x_copy(p, j, 0, quarter(p), quarter(p), to_right, from_left, right)

    def hop_left(p, j):
        return x_copy(p, j, 0, 2 * quarter(p), quarter(p), to_left, from_right, left)

    def pass_right(p, j):
        return x_copy(p, j, quarter(p), 3 * quarter(p), quarter(p) // 2, on_right, opp_left, right)

    def pass_left(p, j):
        n = quarter(p) // 2
        return x_copy(p, j, 5 * n, 7 * n, n, on_left, opp_right, left)

    def select_and_send(p, j):
        n = 0
        for g in PARTS[p]:
            for s in (2 * g, 2 * g + 1):
                parts[p][j, rows * n : rows * n + rows, :] = recv[j][slot_of[s]]
                n += 1
        hop_right(p, j).start()
        hop_left(p, j).start()

    def pass_on(p, j):
        hop_right(p, j).wait_recv()
        pass_right(p, j).start()
        hop_left(p, j).wait_recv()
        pass_left(p, j).start()

    def project_first(p):
        def body(i, carry):
            r = pl.ds(pl.multiple_of(i * quarter(p), quarter(p)), quarter(p))
            lhs = jnp.concatenate([parts[p][j, r, :] for j in range(6)], axis=1)
            accs[p][r, 0:512] = jnp.dot(lhs, wk[0 : COL * 6, :], preferred_element_type=jnp.float32)
            accs[p][r, 512:1024] = jnp.dot(lhs, wv[0 : COL * 6, :], preferred_element_type=jnp.float32)
            return carry

        lax.fori_loop(0, 4, body, 0)

    def project_last(p):
        def body(i, carry):
            r = pl.ds(pl.multiple_of(i * quarter(p), quarter(p)), quarter(p))
            to = pl.ds(pl.multiple_of(i * 2 * rows, 2 * rows), 2 * rows)
            lhs = parts[p][6, r, :]
            k = accs[p][r, 0:512] + jnp.dot(lhs, wk[COL * 6 : COL * 7, :], preferred_element_type=jnp.float32)
            v = accs[p][r, 512:1024] + jnp.dot(lhs, wv[COL * 6 : COL * 7, :], preferred_element_type=jnp.float32)
            k = k.astype(jnp.bfloat16)
            v = v.astype(jnp.bfloat16)
            for n, g in enumerate(PARTS[p]):
                keys[g, to, :] = k[2 * rows * n : 2 * rows * (n + 1), :]
                for m in range(4):
                    values[g, to, 2 * DH * m : 2 * DH * m + DH] = v[
                        2 * rows * n : 2 * rows * (n + 1), DH * m : DH * m + DH
                    ]
            return carry

        lax.fori_loop(0, 4, body, 0)

    def attend(p):
        first = PARTS[p][0]
        heads = [slice(DH * n, DH * n + DH) for n in range(4)]
        wider = [slice(2 * DH * n, 2 * DH * n + 2 * DH) for n in range(4)]

        def block(i):
            return pl.ds(pl.multiple_of(64 * (i + first) + 64, 64), 64)

        def score(i, carry):
            for n in range(4):
                scores[i, n] = lax.dot_general(
                    q_pad[block(i), heads[n]], keys[i + first, :, heads[n]], (((1,), (1,)), ((), ())),
                    preferred_element_type=jnp.float32,
                )
            return carry

        def weigh(i, carry):
            for n in range(4):
                one = scores[i, n]
                top = jnp.max(one, axis=-1, keepdims=True)
                weights[i, n] = jnp.exp2((one - top) * EXP2_SCALE).astype(jnp.bfloat16)
            return carry

        def mix(i, carry):
            for n in range(4):
                both = jnp.dot(weights[i, n], values[i + first, :, wider[n]], preferred_element_type=jnp.float32)
                wide[block(i), heads[n]] = both[:, :DH] / both[:, DH:]
            return carry

        for step in (score, weigh, mix):
            lax.fori_loop(0, len(PARTS[p]), step, 0, unroll=True)

    edge_o = pltpu.make_async_remote_copy(
        src_ref=o_out, dst_ref=o_in, send_sem=edge_send.at[1], recv_sem=edge_recv.at[1],
        device_id=ahead, device_id_type=MESH,
    )

    def write_out(blocks):
        for i in blocks:
            o_ref[0, 64 * i : 64 * i + 64, :] = wide[64 * i + 1 : 64 * i + 65, :].astype(jnp.bfloat16)

    done = [0] * len(PARTS)

    def landed(p, j):
        pass_right(p, j).wait_recv()
        pass_left(p, j).wait_recv()
        done[p] += 1
        if done[p] == 6:
            if p == 0:
                loads[2].wait()
                loads[3].wait()
            project_first(p)
        if done[p] == 7:
            project_last(p)
            if p == 0:
                edge_q.wait_recv()
                row = lax.broadcasted_iota(jnp.int32, (64, 512), 0)
                q_pad[512:576, :] = jnp.where(
                    row == 0, q_pad[512:576, :].astype(jnp.float32), q_in[...].astype(jnp.float32)
                ).astype(jnp.bfloat16)
            attend(p)
            if p == 0:
                o_out[...] = wide[512:576, :].astype(jnp.bfloat16)
                edge_o.start()
                write_out((5, 6, 7))

    for j in SERVE[:UPFRONT]:
        serve(j)
    served = UPFRONT
    seen = set()
    for n in range(len(UNITS) + 2 * LOOK):
        if n < len(UNITS):
            p, j = UNITS[n]
            if j not in seen:
                seen.add(j)
                pltpu.make_async_copy(recv[j], recv[j], serve_recv.at[j]).wait()
            select_and_send(p, j)
            if served < len(SERVE):
                serve(SERVE[served])
                served += 1
        if 0 <= n - LOOK < len(UNITS):
            pass_on(*UNITS[n - LOOK])
        if 0 <= n - 2 * LOOK < len(UNITS):
            if n - 2 * LOOK == len(UNITS) - 1:
                edge_q.wait_send()
                edge_o.wait_send()
                for i, asked in enumerate((asked_y, asked_z)):
                    pltpu.make_async_copy(asked.at[pl.ds(0, 15)], asked.at[pl.ds(0, 15)], tab_send.at[i]).wait()
                pltpu.make_async_copy(e_line.at[pl.ds(0, 7)], e_line.at[pl.ds(0, 7)], pre_send.at[0]).wait()

                @pl.when(y != z)
                def _():
                    spread(0, 1).wait_send()

                for j in SERVE:
                    sent = packed.at[j, pl.ds(1, 15)]
                    pltpu.make_async_copy(sent, sent, serve_send.at[j]).wait()
                for p, j in UNITS:
                    hop_right(p, j).wait_send()
                    hop_left(p, j).wait_send()
                    pass_right(p, j).wait_send()
                    pass_left(p, j).wait_send()
                edge_o.wait_recv()
                wide[0:64, :] = jnp.where(z == 0, 0.0, o_in[...].astype(jnp.float32))
            landed(*UNITS[n - 2 * LOOK])
    write_out((0, 1, 2, 3, 4))


def local(queries, neighbour_ids, encoded, key_weight, value_weight):
    bf16, f32, i32 = jnp.bfloat16, jnp.float32, jnp.int32
    hbm = pl.BlockSpec(memory_space=pl.ANY)
    dma = pltpu.SemaphoreType.DMA
    part_rows = [256 * len(groups) for groups in PARTS]
    return pl.pallas_call(
        exchange_kernel,
        out_shape=jax.ShapeDtypeStruct(queries.shape, bf16),
        in_specs=[pl.BlockSpec(memory_space=pltpu.SMEM), hbm, hbm, hbm, hbm],
        out_specs=pl.BlockSpec(memory_space=pltpu.VMEM),
        scratch_shapes=[
            pltpu.VMEM((512, 512), bf16),
            pltpu.VMEM((8, 32, 896), bf16),
            pltpu.VMEM((8, 32, COL * len(Z_CHUNKS)), bf16),
            pltpu.VMEM((896, 512), bf16),
            pltpu.VMEM((896, 512), bf16),
            pltpu.VMEM((1, 128), i32),
            pltpu.VMEM((16, 1, 128), i32),
            pltpu.VMEM((16, 1, 128), i32),
            pltpu.SMEM((16, 1, 128), i32),
            pltpu.SMEM((16, 1, 128), i32),
            pltpu.VMEM((7, 16, 2, 32, 128), bf16),
            pltpu.VMEM((584, 512), f32),
            pltpu.VMEM((576, 512), bf16),
            pltpu.VMEM((64, 512), bf16),
            pltpu.VMEM((64, 512), bf16),
            pltpu.VMEM((64, 512), bf16),
            pltpu.VMEM((8, 256, 512), bf16),
            pltpu.VMEM((8, 256, 1024), bf16),
            pltpu.VMEM((4, 4, 64, 256), f32),
            pltpu.VMEM((4, 4, 64, 256), bf16),
        ]
        + [pltpu.VMEM((n, 1024), f32) for n in part_rows]
        + [pltpu.VMEM((7, n, COL), bf16) for n in part_rows]
        + [pltpu.VMEM((32, 32, 128), bf16) for _ in range(7)]
        + [dma((4,)), dma((2,)), dma((2,)), dma((2,)), dma((2,)), dma, dma((7,)), dma((7,))]
        + [dma((len(PARTS), 7)) for _ in range(8)]
        + [dma((2,)), dma((2,))],
        compiler_params=pltpu.CompilerParams(
            collective_id=0, has_side_effects=True, vmem_limit_bytes=60 * 2**20
        ),
        cost_estimate=pl.CostEstimate(flops=4_100_000_000, bytes_accessed=6_000_000, transcendentals=600_000),
    )(jnp.transpose(neighbour_ids, (0, 2, 1)), queries, encoded, key_weight, value_weight)


def solution(mesh):
    return jax.shard_map(
        local,
        mesh=mesh,
        in_specs=(
            P("batch", "seq", "mp"),
            P("batch", "seq", None),
            P("batch", None, None),
            P(None, "mp"),
            P(None, "mp"),
        ),
        out_specs=P("batch", "seq", "mp"),
        check_vma=False,
    )
```

```python
import jax
import jax.numpy as jnp
from jax import lax
from jax.experimental import pallas as pl
from jax.experimental.pallas import tpu as pltpu
from jax.sharding import PartitionSpec as P

MESH = pl.DeviceIdType.MESH
DH = 128
EXP2_SCALE = DH ** (-0.5) * 1.4426950408889634
COL = 128
PIECES = ((0, 0), (0, 1), (1, None), (2, None), (6, None), (3, None), (4, None), (5, None))
Y_PIECES = 5
Z_FIRST = 3
Z_COUNT = 3
SERVE = (0, 1, 2, 5, 3, 6, 7, 4)
PARTS = ((4, 5, 6, 7), (0, 1, 2, 3))
UNITS = ((0, 0), (1, 0), (0, 1), (1, 1), (0, 5), (0, 2), (1, 5), (0, 6), (0, 3), (0, 7), (1, 2), (0, 4), (1, 6), (1, 3), (1, 7), (1, 4))
PASS_LAG = 4
SEE_LAG = 8


def make_plan():
    plan = [("serve", i) for i in SERVE]
    for n in range(len(UNITS) + SEE_LAG):
        if 0 <= n - PASS_LAG < len(UNITS):
            plan.append(("pass",) + UNITS[n - PASS_LAG])
        if n < len(UNITS):
            plan.append(("take",) + UNITS[n])
        if n >= SEE_LAG:
            plan.append(("see",) + UNITS[n - SEE_LAG])
    return plan


PLAN = make_plan()


def exchange_kernel(
    ids, q_hbm, e_hbm, wk_hbm, wv_hbm, o_ref,
    q_raw, e_own, e_line, wk, wv, table, asked_y, asked_z, asked_y_s, asked_z_s, wide, q_pad, q_in, o_out, o_in,
    keys, values, scores, weights, acc0, acc1, part0, part1, r0, r1, r2, r3, r4, r5, r6, r7,
    d0, d1, d2, d3, d4, d5, d6, d7,
    load_sem, tab_send, tab_recv, tab_local, pre_send, pre_recv, serve_send, serve_recv,
    to_right, to_left, from_left, from_right, on_right, on_left, opp_left, opp_right, edge_send, edge_recv,
):
    recv = (r0, r1, r2, r3, r4, r5, r6, r7)
    packed = (d0, d1, d2, d3, d4, d5, d6, d7)
    parts = (part0, part1)
    accs = (acc0, acc1)
    z = lax.axis_index("seq")
    b = lax.axis_index("batch")
    x = lax.axis_index("mp")
    y = lax.div(b, 2)
    core = lax.rem(b, 2)
    zc = 2 * z + core
    rows = e_own.shape[1]
    right = (z, b, lax.rem(x + 1, 4))
    left = (z, b, lax.rem(x + 3, 4))
    ahead = (lax.rem(z + 1, 8), b, x)
    behind = (lax.rem(z + 7, 8), b, x)

    def y_line(k):
        to = lax.rem(b + k, 16)
        return to, (z, to, x)

    def z_line(k):
        to = lax.rem(zc + k, 16)
        return to, (lax.div(to, 2), 2 * y + lax.rem(to, 2), x)

    barrier = pltpu.get_barrier_semaphore()

    def greet_one(device):
        pl.semaphore_signal(barrier, inc=1, device_id=device, device_id_type=MESH)

    greet_one(right)
    greet_one(left)

    def greet(k, carry):
        greet_one(y_line(k)[1])
        greet_one(z_line(k)[1])
        return carry

    lax.fori_loop(1, 16, greet, 0)

    def greet_source(k, carry):
        greet_one((lax.rem(z + k, 8), zc, x))
        return carry

    lax.fori_loop(1, 8, greet_source, 0)

    @pl.when(y != z)
    def _():
        greet_one((z, zc, x))

    loads = [
        pltpu.make_async_copy(e_hbm.at[:, pl.ds(pl.multiple_of(x * rows, rows), rows), :], e_own, load_sem.at[0]),
        pltpu.make_async_copy(q_hbm.at[0], q_raw, load_sem.at[1]),
        pltpu.make_async_copy(wk_hbm, wk, load_sem.at[2]),
        pltpu.make_async_copy(wv_hbm, wv, load_sem.at[3]),
    ]
    for copy in loads:
        copy.start()

    lane = lax.broadcasted_iota(jnp.int32, (1, 128), 1)
    lane_owner = lax.shift_right_logical(lane, 1)
    lane_slot = lane & 1
    count = jnp.zeros((1, 128), jnp.int32)
    wanted = jnp.zeros((1, 128), jnp.int32)
    owners = []
    slot_of = []
    for s in range(16):
        one = ids[0, s % 2, s // 2]
        owner = lax.shift_right_logical(one, 3)
        same = lane_owner == owner
        wanted = jnp.where(same & (count == lane_slot), one & 7, wanted)
        count = count + same.astype(jnp.int32)
        rank = jnp.int32(0)
        for other in owners:
            rank = rank + (other == owner).astype(jnp.int32)
        owners.append(owner)
        slot_of.append(owner * 2 + jnp.minimum(rank, 1))
    table[...] = wanted
    loads[0].wait()

    pl.semaphore_wait(barrier, 39 + (y != z).astype(jnp.int32))

    def tell(line, asked, n, me):
        def body(k, carry):
            pltpu.make_async_remote_copy(
                src_ref=table, dst_ref=asked.at[me], send_sem=tab_send.at[n], recv_sem=tab_recv.at[n],
                device_id=line(k)[1], device_id_type=MESH,
            ).start()
            return carry

        lax.fori_loop(1, 16, body, 0)
        pltpu.make_async_copy(table, asked.at[me], tab_recv.at[n]).start()

    tell(y_line, asked_y, 0, b)
    tell(z_line, asked_z, 1, zc)

    z_cols = pl.ds(COL * Z_FIRST, COL * Z_COUNT)

    def spread(k, send):
        return pltpu.make_async_remote_copy(
            src_ref=e_own.at[z, :, z_cols], dst_ref=e_line.at[z], send_sem=pre_send.at[send], recv_sem=pre_recv,
            device_id=(y, 2 * lax.rem(y + k, 8) + core, x), device_id_type=MESH,
        )

    def spread_one(k, carry):
        spread(k, 0).start()
        return carry

    lax.fori_loop(1, 8, spread_one, 0)

    @pl.when(y != z)
    def _():
        spread(0, 1).start()

    @pl.when(y == z)
    def _():
        pltpu.make_async_copy(e_own.at[z, :, z_cols], e_line.at[z], pre_recv).start()

    loads[1].wait()
    wide[0:8, :] = jnp.zeros((8, wide.shape[1]), jnp.float32)
    wide[520:584, :] = jnp.zeros((64, wide.shape[1]), jnp.float32)
    for i in range(8):
        wide[8 + 64 * i : 72 + 64 * i, :] = q_raw[64 * i : 64 * i + 64, :].astype(jnp.float32)
    for i in range(9):
        q_pad[64 * i : 64 * i + 64, :] = wide[7 + 64 * i : 71 + 64 * i, :].astype(jnp.bfloat16)
    edge_q = pltpu.make_async_remote_copy(
        src_ref=q_pad.at[pl.ds(0, 64)], dst_ref=q_in, send_sem=edge_send.at[0], recv_sem=edge_recv.at[0],
        device_id=behind, device_id_type=MESH,
    )
    edge_q.start()
    for g in range(8):
        for m in range(4):
            values[g, :, 2 * DH * m + DH : 2 * DH * m + 2 * DH] = jnp.ones((256, DH), jnp.bfloat16)
    scalars = []
    for n, (asked, asked_s) in enumerate(((asked_y, asked_y_s), (asked_z, asked_z_s))):
        scalars.append(pltpu.make_async_copy(asked, asked_s, tab_local.at[n]))

    def know(n, asked):
        pltpu.make_async_copy(asked, asked, tab_recv.at[n]).wait()
        scalars[n].start()
        scalars[n].wait()

    know(0, asked_y)

    def serve(i):
        j, half = PIECES[i]
        if i >= Y_PIECES:
            block, col, asked_s, me, line = e_line, COL * (j - Z_FIRST), asked_z_s, zc, z_line
            if i == Y_PIECES:
                know(1, asked_z)
                pltpu.make_async_copy(e_line, e_line, pre_recv).wait()
        else:
            block, col, asked_s, me, line = e_own, COL * j, asked_y_s, b, y_line
        first, count = (0, rows) if half is None else (half * rows // 2, rows // 2)

        def pack(k, to):
            for t in range(2):
                packed[i][k, t] = block[asked_s[to, 0, 2 * me + t], first : first + count, col : col + COL]

        def body(k, carry):
            to, device = line(k)
            pack(k, to)
            pltpu.make_async_remote_copy(
                src_ref=packed[i].at[k], dst_ref=recv[i].at[pl.ds(2 * me, 2)],
                send_sem=serve_send.at[i], recv_sem=serve_recv.at[i], device_id=device, device_id_type=MESH,
            ).start()
            return carry

        lax.fori_loop(1, 16, body, 0)
        pack(0, me)
        pltpu.make_async_copy(packed[i].at[0], recv[i].at[pl.ds(2 * me, 2)], serve_recv.at[i]).start()

    def x_copy(p, i, src, dst, first, count, send, rcv, device):
        j = PIECES[i][0]
        return pltpu.make_async_remote_copy(
            src_ref=parts[p].at[j, pl.ds(src * quarter(p) + first, count)],
            dst_ref=parts[p].at[j, pl.ds(dst * quarter(p) + first, count)],
            send_sem=send.at[p, i], recv_sem=rcv.at[p, i], device_id=device, device_id_type=MESH,
        )

    def quarter(p):
        return 2 * rows * len(PARTS[p])

    def span(p, i):
        half = PIECES[i][1]
        return (0, quarter(p)) if half is None else (half * quarter(p) // 2, quarter(p) // 2)

    def hop_right(p, i):
        return x_copy(p, i, 0, 1, *span(p, i), to_right, from_left, right)

    def hop_left(p, i):
        return x_copy(p, i, 0, 2, *span(p, i), to_left, from_right, left)

    def pass_right(p, i):
        first, count = span(p, i)
        return x_copy(p, i, 1, 3, first, count // 2, on_right, opp_left, right)

    def pass_left(p, i):
        first, count = span(p, i)
        return x_copy(p, i, 2, 3, first + count // 2, count // 2, on_left, opp_right, left)

    def select_and_send(p, i):
        j, half = PIECES[i]
        n = 0
        for g in PARTS[p]:
            for s in (2 * g, 2 * g + 1):
                one = recv[i][slot_of[s]]
                for h in (0, 1) if half is None else (half,):
                    at = h * quarter(p) // 2 + rows // 2 * n
                    low = rows // 2 * h if half is None else 0
                    parts[p][j, at : at + rows // 2, :] = one[low : low + rows // 2, :]
                n += 1
        hop_right(p, i).start()
        hop_left(p, i).start()

    def pass_on(p, i):
        hop_right(p, i).wait_recv()
        pass_right(p, i).start()
        hop_left(p, i).wait_recv()
        pass_left(p, i).start()

    def project_first(p):
        def body(i, carry):
            r = pl.ds(pl.multiple_of(i * quarter(p), quarter(p)), quarter(p))
            lhs = jnp.concatenate([parts[p][j, r, :] for j in range(6)], axis=1)
            accs[p][r, 0:512] = jnp.dot(lhs, wk[0 : COL * 6, :], preferred_element_type=jnp.float32)
            accs[p][r, 512:1024] = jnp.dot(lhs, wv[0 : COL * 6, :], preferred_element_type=jnp.float32)
            return carry

        lax.fori_loop(0, 4, body, 0)

    def project_last(p):
        def body(i, carry):
            r = pl.ds(pl.multiple_of(i * quarter(p), quarter(p)), quarter(p))
            lhs = parts[p][6, r, :]
            k = accs[p][r, 0:512] + jnp.dot(lhs, wk[COL * 6 : COL * 7, :], preferred_element_type=jnp.float32)
            v = accs[p][r, 512:1024] + jnp.dot(lhs, wv[COL * 6 : COL * 7, :], preferred_element_type=jnp.float32)
            k = k.astype(jnp.bfloat16)
            v = v.astype(jnp.bfloat16)
            for h in range(2):
                to = pl.ds(pl.multiple_of(2 * rows * i + rows * h, rows), rows)
                for n, g in enumerate(PARTS[p]):
                    at = h * quarter(p) // 2 + rows * n
                    keys[g, to, :] = k[at : at + rows, :]
                    for m in range(4):
                        values[g, to, 2 * DH * m : 2 * DH * m + DH] = v[at : at + rows, DH * m : DH * m + DH]
            return carry

        lax.fori_loop(0, 4, body, 0)

    def attend(p):
        first = PARTS[p][0]
        heads = [slice(DH * n, DH * n + DH) for n in range(4)]
        wider = [slice(2 * DH * n, 2 * DH * n + 2 * DH) for n in range(4)]

        def block(i):
            return pl.ds(pl.multiple_of(64 * (i + first) + 64, 64), 64)

        def score(i, carry):
            for n in range(4):
                scores[i, n] = lax.dot_general(
                    q_pad[block(i), heads[n]], keys[i + first, :, heads[n]], (((1,), (1,)), ((), ())),
                    preferred_element_type=jnp.float32,
                )
            return carry

        def weigh(i, carry):
            for n in range(4):
                one = scores[i, n]
                top = jnp.max(one, axis=-1, keepdims=True)
                weights[i, n] = jnp.exp2((one - top) * EXP2_SCALE).astype(jnp.bfloat16)
            return carry

        def mix(i, carry):
            for n in range(4):
                both = jnp.dot(weights[i, n], values[i + first, :, wider[n]], preferred_element_type=jnp.float32)
                wide[block(i), heads[n]] = both[:, :DH] / both[:, DH:]
            return carry

        for step in (score, weigh, mix):
            lax.fori_loop(0, len(PARTS[p]), step, 0, unroll=True)

    edge_o = pltpu.make_async_remote_copy(
        src_ref=o_out, dst_ref=o_in, send_sem=edge_send.at[1], recv_sem=edge_recv.at[1],
        device_id=ahead, device_id_type=MESH,
    )

    def write_out(blocks):
        for i in blocks:
            o_ref[0, 64 * i : 64 * i + 64, :] = wide[64 * i + 1 : 64 * i + 65, :].astype(jnp.bfloat16)

    done = [0] * len(PARTS)

    def landed(p, j):
        pass_right(p, j).wait_recv()
        pass_left(p, j).wait_recv()
        done[p] += 1
        if done[p] == len(PIECES) - 1:
            if p == 0:
                loads[2].wait()
                loads[3].wait()
            project_first(p)
        if done[p] == len(PIECES):
            project_last(p)
            if p == 0:
                edge_q.wait_recv()
                row = lax.broadcasted_iota(jnp.int32, (64, 512), 0)
                q_pad[512:576, :] = jnp.where(
                    row == 0, q_pad[512:576, :].astype(jnp.float32), q_in[...].astype(jnp.float32)
                ).astype(jnp.bfloat16)
            attend(p)
            if p == 0:
                o_out[...] = wide[512:576, :].astype(jnp.bfloat16)
                edge_o.start()
                write_out((5, 6, 7))

    def drain():
        edge_q.wait_send()
        edge_o.wait_send()
        for i, asked in enumerate((asked_y, asked_z)):
            pltpu.make_async_copy(asked.at[pl.ds(0, 15)], asked.at[pl.ds(0, 15)], tab_send.at[i]).wait()
        pltpu.make_async_copy(e_line.at[pl.ds(0, 7)], e_line.at[pl.ds(0, 7)], pre_send.at[0]).wait()

        @pl.when(y != z)
        def _():
            spread(0, 1).wait_send()

        for i in SERVE:
            sent = packed[i].at[pl.ds(1, 15)]
            pltpu.make_async_copy(sent, sent, serve_send.at[i]).wait()
        for p, i in UNITS:
            hop_right(p, i).wait_send()
            hop_left(p, i).wait_send()
            pass_right(p, i).wait_send()
            pass_left(p, i).wait_send()
        edge_o.wait_recv()
        wide[0:64, :] = jnp.where(z == 0, 0.0, o_in[...].astype(jnp.float32))

    seen = set()
    for step in PLAN:
        if step[0] == "serve":
            serve(step[1])
        elif step[0] == "take":
            p, j = step[1:]
            if j not in seen:
                seen.add(j)
                pltpu.make_async_copy(recv[j], recv[j], serve_recv.at[j]).wait()
            select_and_send(p, j)
        elif step[0] == "pass":
            pass_on(*step[1:])
        else:
            if step[1:] == UNITS[-1]:
                drain()
            landed(*step[1:])
    write_out((0, 1, 2, 3, 4))


def local(queries, neighbour_ids, encoded, key_weight, value_weight):
    bf16, f32, i32 = jnp.bfloat16, jnp.float32, jnp.int32
    hbm = pl.BlockSpec(memory_space=pl.ANY)
    dma = pltpu.SemaphoreType.DMA
    piece_rows = [32 if half is None else 16 for _, half in PIECES]
    part_rows = [256 * len(groups) for groups in PARTS]
    return pl.pallas_call(
        exchange_kernel,
        out_shape=jax.ShapeDtypeStruct(queries.shape, bf16),
        in_specs=[pl.BlockSpec(memory_space=pltpu.SMEM), hbm, hbm, hbm, hbm],
        out_specs=pl.BlockSpec(memory_space=pltpu.VMEM),
        scratch_shapes=[
            pltpu.VMEM((512, 512), bf16),
            pltpu.VMEM((8, 32, 896), bf16),
            pltpu.VMEM((8, 32, COL * Z_COUNT), bf16),
            pltpu.VMEM((896, 512), bf16),
            pltpu.VMEM((896, 512), bf16),
            pltpu.VMEM((1, 128), i32),
            pltpu.VMEM((16, 1, 128), i32),
            pltpu.VMEM((16, 1, 128), i32),
            pltpu.SMEM((16, 1, 128), i32),
            pltpu.SMEM((16, 1, 128), i32),
            pltpu.VMEM((584, 512), f32),
            pltpu.VMEM((576, 512), bf16),
            pltpu.VMEM((64, 512), bf16),
            pltpu.VMEM((64, 512), bf16),
            pltpu.VMEM((64, 512), bf16),
            pltpu.VMEM((8, 256, 512), bf16),
            pltpu.VMEM((8, 256, 1024), bf16),
            pltpu.VMEM((5, 4, 64, 256), f32),
            pltpu.VMEM((5, 4, 64, 256), bf16),
        ]
        + [pltpu.VMEM((n, 1024), f32) for n in part_rows]
        + [pltpu.VMEM((7, n, COL), bf16) for n in part_rows]
        + [pltpu.VMEM((32, n, COL), bf16) for n in piece_rows]
        + [pltpu.VMEM((16, 2, n, COL), bf16) for n in piece_rows]
        + [dma((4,)), dma((2,)), dma((2,)), dma((2,)), dma((2,)), dma, dma((8,)), dma((8,))]
        + [dma((len(PARTS), 8)) for _ in range(8)]
        + [dma((2,)), dma((2,))],
        compiler_params=pltpu.CompilerParams(
            collective_id=0, has_side_effects=True, vmem_limit_bytes=53 * 2**20
        ),
        cost_estimate=pl.CostEstimate(flops=4_100_000_000, bytes_accessed=6_000_000, transcendentals=600_000),
    )(jnp.transpose(neighbour_ids, (0, 2, 1)), queries, encoded, key_weight, value_weight)


def solution(mesh):
    return jax.shard_map(
        local,
        mesh=mesh,
        in_specs=(
            P("batch", "seq", "mp"),
            P("batch", "seq", None),
            P("batch", None, None),
            P(None, "mp"),
            P(None, "mp"),
        ),
        out_specs=P("batch", "seq", "mp"),
        check_vma=False,
    )
```

```python
import jax
import jax.numpy as jnp
from jax import lax
from jax.experimental import pallas as pl
from jax.experimental.pallas import tpu as pltpu
from jax.sharding import PartitionSpec as P

MESH = pl.DeviceIdType.MESH
DH = 128
EXP2_SCALE = DH ** (-0.5) * 1.4426950408889634
COL = 128
PIECES = ((0, 0), (0, 1), (1, None), (2, None), (6, None), (3, None), (4, None), (5, None))
Y_PIECES = 5
Z_FIRST = 3
Z_COUNT = 3
SERVE = (0, 1, 2, 5, 3, 6, 7, 4)
PARTS = ((4, 5, 6, 7), (0, 1, 2, 3))
UNITS = ((0, 0), (1, 0), (0, 1), (1, 1), (0, 5), (0, 2), (1, 5), (0, 6), (0, 3), (0, 7), (1, 2), (0, 4), (1, 6), (1, 3), (1, 7), (1, 4))
PASS_LAG = 4
SEE_LAG = 8
SOON_LAG = 6
SOON = 11


def make_plan():
    plan = [("serve", i) for i in SERVE]
    for n in range(len(UNITS) + SEE_LAG):
        if 0 <= n - PASS_LAG < len(UNITS):
            plan.append(("pass",) + UNITS[n - PASS_LAG])
        if n < len(UNITS):
            plan.append(("take",) + UNITS[n])
        if 0 <= n - SOON_LAG < SOON:
            plan.append(("see",) + UNITS[n - SOON_LAG])
        if n - SEE_LAG >= SOON:
            plan.append(("see",) + UNITS[n - SEE_LAG])
    return plan


PLAN = make_plan()


def exchange_kernel(
    ids, q_hbm, e_hbm, wk_hbm, wv_hbm, o_ref,
    q_raw, e_own, e_line, wk, wv, table, asked_y, asked_z, asked_y_s, asked_z_s, wide, q_pad, q_in, o_out, o_in,
    keys, values, scores, weights, acc0, acc1, part0, part1, r0, r1, r2, r3, r4, r5, r6, r7,
    d0, d1, d2, d3, d4, d5, d6, d7,
    load_sem, tab_send, tab_recv, tab_local, pre_send, pre_recv, serve_send, serve_recv,
    to_right, to_left, from_left, from_right, on_right, on_left, opp_left, opp_right, edge_send, edge_recv,
):
    recv = (r0, r1, r2, r3, r4, r5, r6, r7)
    packed = (d0, d1, d2, d3, d4, d5, d6, d7)
    parts = (part0, part1)
    accs = (acc0, acc1)
    z = lax.axis_index("seq")
    b = lax.axis_index("batch")
    x = lax.axis_index("mp")
    y = lax.div(b, 2)
    core = lax.rem(b, 2)
    zc = 2 * z + core
    rows = e_own.shape[1]
    right = (z, b, lax.rem(x + 1, 4))
    left = (z, b, lax.rem(x + 3, 4))
    ahead = (lax.rem(z + 1, 8), b, x)
    behind = (lax.rem(z + 7, 8), b, x)

    def y_line(k):
        to = lax.rem(b + k, 16)
        return to, (z, to, x)

    def z_line(k):
        to = lax.rem(zc + k, 16)
        return to, (lax.div(to, 2), 2 * y + lax.rem(to, 2), x)

    barrier = pltpu.get_barrier_semaphore()

    def greet_one(device):
        pl.semaphore_signal(barrier, inc=1, device_id=device, device_id_type=MESH)

    greet_one(right)
    greet_one(left)

    def greet(k, carry):
        greet_one(y_line(k)[1])
        greet_one(z_line(k)[1])
        return carry

    lax.fori_loop(1, 16, greet, 0)

    def greet_source(k, carry):
        greet_one((lax.rem(z + k, 8), zc, x))
        return carry

    lax.fori_loop(1, 8, greet_source, 0)

    @pl.when(y != z)
    def _():
        greet_one((z, zc, x))

    loads = [
        pltpu.make_async_copy(e_hbm.at[:, pl.ds(pl.multiple_of(x * rows, rows), rows), :], e_own, load_sem.at[0]),
        pltpu.make_async_copy(q_hbm.at[0], q_raw, load_sem.at[1]),
        pltpu.make_async_copy(wk_hbm, wk, load_sem.at[2]),
        pltpu.make_async_copy(wv_hbm, wv, load_sem.at[3]),
    ]
    for copy in loads:
        copy.start()

    lane = lax.broadcasted_iota(jnp.int32, (1, 128), 1)
    lane_owner = lax.shift_right_logical(lane, 1)
    lane_slot = lane & 1
    count = jnp.zeros((1, 128), jnp.int32)
    wanted = jnp.zeros((1, 128), jnp.int32)
    owners = []
    slot_of = []
    for s in range(16):
        one = ids[0, s % 2, s // 2]
        owner = lax.shift_right_logical(one, 3)
        same = lane_owner == owner
        wanted = jnp.where(same & (count == lane_slot), one & 7, wanted)
        count = count + same.astype(jnp.int32)
        rank = jnp.int32(0)
        for other in owners:
            rank = rank + (other == owner).astype(jnp.int32)
        owners.append(owner)
        slot_of.append(owner * 2 + jnp.minimum(rank, 1))
    table[...] = wanted
    loads[0].wait()

    pl.semaphore_wait(barrier, 39 + (y != z).astype(jnp.int32))

    def tell(line, asked, n, me):
        def body(k, carry):
            pltpu.make_async_remote_copy(
                src_ref=table, dst_ref=asked.at[me], send_sem=tab_send.at[n], recv_sem=tab_recv.at[n],
                device_id=line(k)[1], device_id_type=MESH,
            ).start()
            return carry

        lax.fori_loop(1, 16, body, 0)
        pltpu.make_async_copy(table, asked.at[me], tab_recv.at[n]).start()

    tell(y_line, asked_y, 0, b)
    tell(z_line, asked_z, 1, zc)

    z_cols = pl.ds(COL * Z_FIRST, COL * Z_COUNT)

    def spread(k, send):
        return pltpu.make_async_remote_copy(
            src_ref=e_own.at[z, :, z_cols], dst_ref=e_line.at[z], send_sem=pre_send.at[send], recv_sem=pre_recv,
            device_id=(y, 2 * lax.rem(y + k, 8) + core, x), device_id_type=MESH,
        )

    def spread_one(k, carry):
        spread(k, 0).start()
        return carry

    lax.fori_loop(1, 8, spread_one, 0)

    @pl.when(y != z)
    def _():
        spread(0, 1).start()

    @pl.when(y == z)
    def _():
        pltpu.make_async_copy(e_own.at[z, :, z_cols], e_line.at[z], pre_recv).start()

    loads[1].wait()
    wide[0:8, :] = jnp.zeros((8, wide.shape[1]), jnp.float32)
    wide[520:584, :] = jnp.zeros((64, wide.shape[1]), jnp.float32)
    for i in range(8):
        wide[8 + 64 * i : 72 + 64 * i, :] = q_raw[64 * i : 64 * i + 64, :].astype(jnp.float32)
    for i in range(9):
        q_pad[64 * i : 64 * i + 64, :] = wide[7 + 64 * i : 71 + 64 * i, :].astype(jnp.bfloat16)
    edge_q = pltpu.make_async_remote_copy(
        src_ref=q_pad.at[pl.ds(0, 64)], dst_ref=q_in, send_sem=edge_send.at[0], recv_sem=edge_recv.at[0],
        device_id=behind, device_id_type=MESH,
    )
    edge_q.start()
    for g in range(8):
        for m in range(4):
            values[g, :, 2 * DH * m + DH : 2 * DH * m + 2 * DH] = jnp.ones((256, DH), jnp.bfloat16)
    scalars = []
    for n, (asked, asked_s) in enumerate(((asked_y, asked_y_s), (asked_z, asked_z_s))):
        scalars.append(pltpu.make_async_copy(asked, asked_s, tab_local.at[n]))

    def know(n, asked):
        pltpu.make_async_copy(asked, asked, tab_recv.at[n]).wait()
        scalars[n].start()
        scalars[n].wait()

    know(0, asked_y)

    def serve(i):
        j, half = PIECES[i]
        if i >= Y_PIECES:
            block, col, asked_s, me, line = e_line, COL * (j - Z_FIRST), asked_z_s, zc, z_line
            if i == Y_PIECES:
                know(1, asked_z)
                pltpu.make_async_copy(e_line, e_line, pre_recv).wait()
        else:
            block, col, asked_s, me, line = e_own, COL * j, asked_y_s, b, y_line
        first, count = (0, rows) if half is None else (half * rows // 2, rows // 2)

        def pack(k, to):
            for t in range(2):
                packed[i][k, t] = block[asked_s[to, 0, 2 * me + t], first : first + count, col : col + COL]

        def body(k, carry):
            to, device = line(k)
            pack(k, to)
            pltpu.make_async_remote_copy(
                src_ref=packed[i].at[k], dst_ref=recv[i].at[pl.ds(2 * me, 2)],
                send_sem=serve_send.at[i], recv_sem=serve_recv.at[i], device_id=device, device_id_type=MESH,
            ).start()
            return carry

        lax.fori_loop(1, 16, body, 0)
        pack(0, me)
        pltpu.make_async_copy(packed[i].at[0], recv[i].at[pl.ds(2 * me, 2)], serve_recv.at[i]).start()

    def x_copy(p, i, src, dst, first, count, send, rcv, device):
        j = PIECES[i][0]
        return pltpu.make_async_remote_copy(
            src_ref=parts[p].at[j, pl.ds(src * quarter(p) + first, count)],
            dst_ref=parts[p].at[j, pl.ds(dst * quarter(p) + first, count)],
            send_sem=send.at[p, i], recv_sem=rcv.at[p, i], device_id=device, device_id_type=MESH,
        )

    def quarter(p):
        return 2 * rows * len(PARTS[p])

    def span(p, i):
        half = PIECES[i][1]
        return (0, quarter(p)) if half is None else (half * quarter(p) // 2, quarter(p) // 2)

    def hop_right(p, i):
        return x_copy(p, i, 0, 1, *span(p, i), to_right, from_left, right)

    def hop_left(p, i):
        return x_copy(p, i, 0, 2, *span(p, i), to_left, from_right, left)

    def pass_right(p, i):
        first, count = span(p, i)
        return x_copy(p, i, 1, 3, first, count // 2, on_right, opp_left, right)

    def pass_left(p, i):
        first, count = span(p, i)
        return x_copy(p, i, 2, 3, first + count // 2, count // 2, on_left, opp_right, left)

    def select_and_send(p, i):
        j, half = PIECES[i]
        n = 0
        for g in PARTS[p]:
            for s in (2 * g, 2 * g + 1):
                one = recv[i][slot_of[s]]
                for h in (0, 1) if half is None else (half,):
                    at = h * quarter(p) // 2 + rows // 2 * n
                    low = rows // 2 * h if half is None else 0
                    parts[p][j, at : at + rows // 2, :] = one[low : low + rows // 2, :]
                n += 1
        hop_right(p, i).start()
        hop_left(p, i).start()

    def pass_on(p, i):
        hop_right(p, i).wait_recv()
        pass_right(p, i).start()
        hop_left(p, i).wait_recv()
        pass_left(p, i).start()

    def project_first(p):
        def body(i, carry):
            r = pl.ds(pl.multiple_of(i * quarter(p), quarter(p)), quarter(p))
            lhs = jnp.concatenate([parts[p][j, r, :] for j in range(6)], axis=1)
            accs[p][r, 0:512] = jnp.dot(lhs, wk[0 : COL * 6, :], preferred_element_type=jnp.float32)
            accs[p][r, 512:1024] = jnp.dot(lhs, wv[0 : COL * 6, :], preferred_element_type=jnp.float32)
            return carry

        lax.fori_loop(0, 4, body, 0)

    def project_last(p):
        def body(i, carry):
            r = pl.ds(pl.multiple_of(i * quarter(p), quarter(p)), quarter(p))
            lhs = parts[p][6, r, :]
            k = accs[p][r, 0:512] + jnp.dot(lhs, wk[COL * 6 : COL * 7, :], preferred_element_type=jnp.float32)
            v = accs[p][r, 512:1024] + jnp.dot(lhs, wv[COL * 6 : COL * 7, :], preferred_element_type=jnp.float32)
            k = k.astype(jnp.bfloat16)
            v = v.astype(jnp.bfloat16)
            for h in range(2):
                to = pl.ds(pl.multiple_of(2 * rows * i + rows * h, rows), rows)
                for n, g in enumerate(PARTS[p]):
                    at = h * quarter(p) // 2 + rows * n
                    keys[g, to, :] = k[at : at + rows, :]
                    for m in range(4):
                        values[g, to, 2 * DH * m : 2 * DH * m + DH] = v[at : at + rows, DH * m : DH * m + DH]
            return carry

        lax.fori_loop(0, 4, body, 0)

    def attend(p):
        first = PARTS[p][0]
        heads = [slice(DH * n, DH * n + DH) for n in range(4)]
        wider = [slice(2 * DH * n, 2 * DH * n + 2 * DH) for n in range(4)]

        def block(i):
            return pl.ds(pl.multiple_of(64 * (i + first) + 64, 64), 64)

        def score(i, carry):
            for n in range(4):
                scores[i, n] = lax.dot_general(
                    q_pad[block(i), heads[n]], keys[i + first, :, heads[n]], (((1,), (1,)), ((), ())),
                    preferred_element_type=jnp.float32,
                )
            return carry

        def weigh(i, carry):
            for n in range(4):
                one = scores[i, n]
                top = jnp.max(one, axis=-1, keepdims=True)
                weights[i, n] = jnp.exp2((one - top) * EXP2_SCALE).astype(jnp.bfloat16)
            return carry

        def mix(i, carry):
            for n in range(4):
                both = jnp.dot(weights[i, n], values[i + first, :, wider[n]], preferred_element_type=jnp.float32)
                wide[block(i), heads[n]] = both[:, :DH] / both[:, DH:]
            return carry

        for step in (score, weigh, mix):
            lax.fori_loop(0, len(PARTS[p]), step, 0, unroll=True)

    edge_o = pltpu.make_async_remote_copy(
        src_ref=o_out, dst_ref=o_in, send_sem=edge_send.at[1], recv_sem=edge_recv.at[1],
        device_id=ahead, device_id_type=MESH,
    )

    def write_out(blocks):
        for i in blocks:
            o_ref[0, 64 * i : 64 * i + 64, :] = wide[64 * i + 1 : 64 * i + 65, :].astype(jnp.bfloat16)

    done = [0] * len(PARTS)

    def landed(p, j):
        pass_right(p, j).wait_recv()
        pass_left(p, j).wait_recv()
        done[p] += 1
        if done[p] == len(PIECES) - 1:
            if p == 0:
                loads[2].wait()
                loads[3].wait()
            project_first(p)
        if done[p] == len(PIECES):
            project_last(p)
            if p == 0:
                edge_q.wait_recv()
                row = lax.broadcasted_iota(jnp.int32, (64, 512), 0)
                q_pad[512:576, :] = jnp.where(
                    row == 0, q_pad[512:576, :].astype(jnp.float32), q_in[...].astype(jnp.float32)
                ).astype(jnp.bfloat16)
            attend(p)
            if p == 0:
                o_out[...] = wide[512:576, :].astype(jnp.bfloat16)
                edge_o.start()
                write_out((5, 6, 7))

    def drain():
        edge_q.wait_send()
        edge_o.wait_send()
        for i, asked in enumerate((asked_y, asked_z)):
            pltpu.make_async_copy(asked.at[pl.ds(0, 15)], asked.at[pl.ds(0, 15)], tab_send.at[i]).wait()
        pltpu.make_async_copy(e_line.at[pl.ds(0, 7)], e_line.at[pl.ds(0, 7)], pre_send.at[0]).wait()

        @pl.when(y != z)
        def _():
            spread(0, 1).wait_send()

        for i in SERVE:
            sent = packed[i].at[pl.ds(1, 15)]
            pltpu.make_async_copy(sent, sent, serve_send.at[i]).wait()
        for p, i in UNITS:
            hop_right(p, i).wait_send()
            hop_left(p, i).wait_send()
            pass_right(p, i).wait_send()
            pass_left(p, i).wait_send()
        edge_o.wait_recv()
        wide[0:64, :] = jnp.where(z == 0, 0.0, o_in[...].astype(jnp.float32))

    seen = set()
    for step in PLAN:
        if step[0] == "serve":
            serve(step[1])
        elif step[0] == "take":
            p, j = step[1:]
            if j not in seen:
                seen.add(j)
                pltpu.make_async_copy(recv[j], recv[j], serve_recv.at[j]).wait()
            select_and_send(p, j)
        elif step[0] == "pass":
            pass_on(*step[1:])
        else:
            if step[1:] == UNITS[-1]:
                drain()
            landed(*step[1:])
    write_out((0, 1, 2, 3, 4))


def local(queries, neighbour_ids, encoded, key_weight, value_weight):
    bf16, f32, i32 = jnp.bfloat16, jnp.float32, jnp.int32
    hbm = pl.BlockSpec(memory_space=pl.ANY)
    dma = pltpu.SemaphoreType.DMA
    piece_rows = [32 if half is None else 16 for _, half in PIECES]
    part_rows = [256 * len(groups) for groups in PARTS]
    return pl.pallas_call(
        exchange_kernel,
        out_shape=jax.ShapeDtypeStruct(queries.shape, bf16),
        in_specs=[pl.BlockSpec(memory_space=pltpu.SMEM), hbm, hbm, hbm, hbm],
        out_specs=pl.BlockSpec(memory_space=pltpu.VMEM),
        scratch_shapes=[
            pltpu.VMEM((512, 512), bf16),
            pltpu.VMEM((8, 32, 896), bf16),
            pltpu.VMEM((8, 32, COL * Z_COUNT), bf16),
            pltpu.VMEM((896, 512), bf16),
            pltpu.VMEM((896, 512), bf16),
            pltpu.VMEM((1, 128), i32),
            pltpu.VMEM((16, 1, 128), i32),
            pltpu.VMEM((16, 1, 128), i32),
            pltpu.SMEM((16, 1, 128), i32),
            pltpu.SMEM((16, 1, 128), i32),
            pltpu.VMEM((584, 512), f32),
            pltpu.VMEM((576, 512), bf16),
            pltpu.VMEM((64, 512), bf16),
            pltpu.VMEM((64, 512), bf16),
            pltpu.VMEM((64, 512), bf16),
            pltpu.VMEM((8, 256, 512), bf16),
            pltpu.VMEM((8, 256, 1024), bf16),
            pltpu.VMEM((5, 4, 64, 256), f32),
            pltpu.VMEM((5, 4, 64, 256), bf16),
        ]
        + [pltpu.VMEM((n, 1024), f32) for n in part_rows]
        + [pltpu.VMEM((7, n, COL), bf16) for n in part_rows]
        + [pltpu.VMEM((32, n, COL), bf16) for n in piece_rows]
        + [pltpu.VMEM((16, 2, n, COL), bf16) for n in piece_rows]
        + [dma((4,)), dma((2,)), dma((2,)), dma((2,)), dma((2,)), dma, dma((8,)), dma((8,))]
        + [dma((len(PARTS), 8)) for _ in range(8)]
        + [dma((2,)), dma((2,))],
        compiler_params=pltpu.CompilerParams(
            collective_id=0, has_side_effects=True, vmem_limit_bytes=53 * 2**20
        ),
        cost_estimate=pl.CostEstimate(flops=4_100_000_000, bytes_accessed=6_000_000, transcendentals=600_000),
    )(jnp.transpose(neighbour_ids, (0, 2, 1)), queries, encoded, key_weight, value_weight)


def solution(mesh):
    return jax.shard_map(
        local,
        mesh=mesh,
        in_specs=(
            P("batch", "seq", "mp"),
            P("batch", "seq", None),
            P("batch", None, None),
            P(None, "mp"),
            P(None, "mp"),
        ),
        out_specs=P("batch", "seq", "mp"),
        check_vma=False,
    )
```
